128 devices in a mesh: wa: 8 (over z, core), grid: 16 (over y, x).
Axes of the slice: x: 4, y: 4, z: 4, core: 2. Of those that a mesh axis runs over, the one named last changes fastest.
Arguments:
- jones: bfloat16 [32, 4, 2, 512, 512], P('wa', None, None, 'grid'), may hold values from -6 to 6
- owner: int32 [32], replicated, may hold values from 0 to 31, each once
- mask: int32 [3, 4, 4], replicated, may hold values 0 or 1
- w_operator: bfloat16 [16, 2, 512, 512], P('wa', None, 'grid'), may hold values from -0.1875 to 0.1875
Outputs:
- conv: bfloat16 [512, 16, 3, 16, 2, 512], P('grid', 'wa')
The draws below stay inside these ranges and needn't reach their ends.
Inputs may be any that keep to these rules, and one draw needn't show every extreme that they name: owner[t] is the slot that holds type t; every slot holds exactly one type.
All inputs are finite; a program needn't handle non-finite values.
Results may differ from the reference program's by a relative error of at most 0.0058.
Values may be sent and summed in bfloat16 or wider, within the bound.
No kernel may reach another device: no remote copies, remote signals or barrier semaphores. Data moves between devices by JAX's collectives and lax.ppermute only.
A program may use at most 576 MiB of HBM per device.

```python
import jax
import jax.numpy as jnp
import numpy as np
from jax import lax

G = 512
TYPES_RUN = 3
TYPES = 32
WPLANES = 16


def touch_ends(values, stream_key, least, top_value):
    spot = [jax.random.randint(jax.random.fold_in(stream_key, axis), (), 0, length) for axis, length in enumerate(values.shape)]
    widest = values.shape.index(max(values.shape))
    beside = spot[:widest] + [(spot[widest] + 1) % values.shape[widest]] + spot[widest + 1:]
    return values.at[tuple(spot)].set(least).at[tuple(beside)].set(top_value)


def shard_levels(own_key, shape, cuts, smallest, high):
    def one(axis_at, shards_of):
        heights = jax.random.uniform(jax.random.fold_in(jax.random.fold_in(own_key, 6), axis_at), (shards_of,), jnp.float32, smallest / len(cuts), high / len(cuts))
        return jnp.repeat(jnp.exp(heights), shape[axis_at] // shards_of).reshape((-1,) + (1,) * (len(shape) - axis_at - 1))

    gain = one(*cuts[0])
    for cut in cuts[1:]:
        gain = gain * one(*cut)
    return gain


def bell_draw(stream_key, shape, deviation, most, split=(), dtype=jnp.bfloat16):
    drawn = deviation * jax.random.normal(stream_key, shape, jnp.float32)
    if split:
        drawn = drawn * shard_levels(stream_key, shape, split, -0.22, 0.18)
    return jnp.clip(drawn, -most, most).astype(dtype)


def setup_inputs(seed: int = 0) -> dict:
    seeds = jax.random.split(jax.random.key(seed), 5)
    jones = bell_draw(seeds[0], (TYPES, 4, 2, G, G), 1.0, 6.0, ((0, 8), (3, 16)))
    owner = jax.random.permutation(seeds[1], TYPES).astype(jnp.int32)
    mask = touch_ends((jax.random.randint(seeds[2], (TYPES_RUN, 4, 4), 0, 4) < 3).astype(jnp.int32), jax.random.fold_in(seeds[2], 1), 0, 1)
    w_operator = bell_draw(seeds[3], (WPLANES, 2, G, G), (2 * G) ** -0.5, 0.1875, ((0, 8), (2, 16)))
    return dict(jones=jones, owner=owner, mask=mask, w_operator=w_operator)


def term_tables():
    first = np.array([2 * (entry // 8) + (entry // 2) % 2 for entry in range(16)])
    second = np.array([2 * ((entry // 4) % 2) + entry % 2 for entry in range(16)])
    return first, second


def reference(jones, owner, mask, w_operator):
    high = lax.Precision.HIGHEST
    first, second = term_tables()
    per_type = []
    for index in range(TYPES_RUN):
        local = jones[owner[index]].astype(jnp.float32)
        left = local[first]
        right = local[second]
        real = left[:, 0] * right[:, 0] + left[:, 1] * right[:, 1]
        imag = left[:, 1] * right[:, 0] - left[:, 0] * right[:, 1]
        weights = mask[index].reshape(16).astype(jnp.float32)
        mueller = (jnp.stack([real, imag], 1) * weights[:, None, None, None]).astype(jnp.bfloat16)
        mueller = lax.optimization_barrier(mueller).astype(jnp.float32)
        planes = []
        for plane in range(WPLANES):
            kreal = w_operator[plane, 0].astype(jnp.float32)
            kimag = w_operator[plane, 1].astype(jnp.float32)
            yreal = jnp.einsum('elm,vm->elv', mueller[:, 0], kreal, precision=high) - jnp.einsum('elm,vm->elv', mueller[:, 1], kimag, precision=high)
            yimag = jnp.einsum('elm,vm->elv', mueller[:, 0], kimag, precision=high) + jnp.einsum('elm,vm->elv', mueller[:, 1], kreal, precision=high)
            rowt = jnp.stack([yreal, yimag], 1).astype(jnp.bfloat16)
            rowt = lax.optimization_barrier(rowt).astype(jnp.float32)
            creal = jnp.einsum('ul,elv->uev', kreal, rowt[:, 0], precision=high) - jnp.einsum('ul,elv->uev', kimag, rowt[:, 1], precision=high)
            cimag = jnp.einsum('ul,elv->uev', kreal, rowt[:, 1], precision=high) + jnp.einsum('ul,elv->uev', kimag, rowt[:, 0], precision=high)
            planes.append(jnp.stack([creal, cimag], 2).astype(jnp.bfloat16))
        per_type.append(jnp.stack(planes, 1))
    return jnp.stack(per_type, 2)
```

```python
import jax
import jax.numpy as jnp
import numpy as np
from jax import lax
from jax.experimental import pallas as pl
from jax.experimental.pallas import tpu as pltpu
from jax.sharding import PartitionSpec as P

RUN = 3
G = 512
ROWS = 32
PLANES = 2

CLASSES = (((1, 3, 4, 12), (3, 4, 12, 1)), ((4, 12, 1, 3), (12, 1, 3, 4)))
ZCLASSES = ((2, 6), (6, 2))

PAIRS = ((0, 1), (0, 2), (0, 3), (1, 2), (1, 3), (2, 3))


def term(a, b):
    return 8 * (a // 2) + 4 * (b // 2) + 2 * (a % 2) + b % 2


def block_masks():
    table = np.zeros((2, 2, 16), np.int32)
    for core in range(2):
        for half in range(2):
            for block in range(16):
                for step in range(4):
                    if block >> step & 1:
                        table[core, half, block] ^= CLASSES[core][half][step]
    return table


def exchange(value, wa_mask, grid_mask):
    perm = []
    for wa in range(8):
        for grid in range(16):
            core = wa % 2
            perm.append((wa * 16 + grid, (wa ^ wa_mask(core)) * 16 + (grid ^ grid_mask(core))))
    return lax.ppermute(value, ("wa", "grid"), perm)


def swap_core(value):
    return exchange(value, lambda core: 1, lambda core: 0)


def swap_z(value, step):
    return exchange(value, lambda core: ZCLASSES[core][step], lambda core: 0)


def swap_grid(value, half, step):
    return exchange(value, lambda core: 0, lambda core: CLASSES[core][half][step])


def transform_kernel(index, *refs):
    (place, keep, ku, k3, k40, k41, own3, own40, own41, far3, far40, far41) = refs[:12]
    out, fields, operator, real, imag, left, staged, field_sem, operator_sem, out_sem = refs[-10:]
    core = place[0]
    own4 = (own40, own41)
    far4 = (far40, far41)
    k4 = (k40, k41)
    for half in range(2):
        for block in range(16):
            row = pl.multiple_of(place[1 + 16 * half + block] * ROWS, ROWS)
            low = block < 8
            source = own3.at[half, block] if low else own4[half].at[block - 8]
            pltpu.make_async_copy(
                source, fields.at[core, pl.ds(2 * half, 2), pl.ds(row, ROWS)], field_sem
            ).start()
            far_row = pl.multiple_of(place[33 + 16 * half + block] * ROWS, ROWS)
            source = far3.at[half, block] if low else far4[half].at[block - 8]
            pltpu.make_async_copy(
                source, fields.at[1 - core, pl.ds(2 * half, 2), pl.ds(far_row, ROWS)], field_sem
            ).start()
    for half in range(2):
        for block in range(16):
            row = pl.multiple_of(place[1 + 16 * half + block] * ROWS, ROWS)
            source = k3.at[half, block] if block < 8 else k4[half].at[block - 8]
            pltpu.make_async_copy(
                source, operator.at[half, :, pl.ds(row, ROWS)], operator_sem
            ).start()
    pltpu.make_async_copy(fields, fields, field_sem).wait()

    def products(a, b, want_imag):
        def chunk(step, carry):
            rows = pl.ds(pl.multiple_of(step * 64, 64), 64)
            ar = fields[0, a, rows].astype(jnp.float32)
            ai = fields[1, a, rows].astype(jnp.float32)
            br = fields[0, b, rows].astype(jnp.float32)
            bi = fields[1, b, rows].astype(jnp.float32)
            real[rows] = (ar * br + ai * bi).astype(jnp.bfloat16)
            if want_imag:
                imag[rows] = (ai * br - ar * bi).astype(jnp.bfloat16)
            return carry

        lax.fori_loop(0, G // 64, chunk, 0)

    def put(plane, entry, scale, value, turned):
        rows = pl.ds(pl.multiple_of(entry * 64, 64), 64)
        left[plane, rows, 0:G] = (value * scale).astype(jnp.bfloat16)
        left[plane, rows, G : 2 * G] = (turned * scale).astype(jnp.bfloat16)

    def pair(a, b):
        products(a, b, True)
        first = 8 * (a // 2) + 4 * (b // 2) + 2 * (a % 2) + b % 2
        second = 8 * (b // 2) + 4 * (a // 2) + 2 * (b % 2) + a % 2
        for plane in range(PLANES):
            rows = slice(plane * 128, plane * 128 + 128)
            pa = jnp.dot(ku[rows], real[...], preferred_element_type=jnp.float32)
            pb = jnp.dot(ku[rows], imag[...], preferred_element_type=jnp.float32)
            put(plane, first, keep[first], pa[:64] + pb[64:], pa[64:] - pb[:64])
            put(plane, second, keep[second], pa[:64] - pb[64:], pa[64:] + pb[:64])

    def square(a):
        products(a, a, False)
        entry = 8 * (a // 2) + 4 * (a // 2) + 2 * (a % 2) + a % 2
        for plane in range(PLANES):
            rows = slice(plane * 128, plane * 128 + 128)
            pa = jnp.dot(ku[rows], real[...], preferred_element_type=jnp.float32)
            put(plane, entry, keep[entry], pa[:64], pa[64:])

    def square_step(a, carry):
        square(a)
        return carry

    def pair_step(step, carry):
        a = jnp.where(step < 3, 0, jnp.where(step < 5, 1, 2))
        b = jnp.where(step < 3, step + 1, jnp.where(step < 5, step - 1, 3))
        pair(a, b)
        return carry

    lax.fori_loop(0, 4, square_step, 0)
    lax.fori_loop(0, 6, pair_step, 0)
    pltpu.make_async_copy(operator, operator, operator_sem).wait()

    contract = (((1,), (1,)), ((), ()))

    for plane in range(PLANES):
        def second_pass(group, carry, plane=plane):
            rows = pl.ds(pl.multiple_of(group * 256, 256), 256)
            total = lax.dot_general(
                left[plane, rows, 0:G], operator[plane, 0], contract, preferred_element_type=jnp.float32
            ) + lax.dot_general(
                left[plane, rows, G : 2 * G], operator[plane, 1], contract, preferred_element_type=jnp.float32
            )
            staged[plane, pl.ds(group * 4, 4)] = total.astype(jnp.bfloat16).reshape(4, ROWS, 2, G)
            for entry in range(4):
                pltpu.make_async_copy(
                    staged.at[plane, group * 4 + entry],
                    out.at[:, plane, index, group * 4 + entry],
                    out_sem,
                ).start()
            return carry

        lax.fori_loop(0, 4, second_pass, 0)
    pltpu.make_async_copy(staged, staged, out_sem).wait()


def transform(index, place, keep, ku, operators, own, far, previous):
    anywhere = pl.BlockSpec(memory_space=pl.ANY)
    scalars = pl.BlockSpec(memory_space=pltpu.SMEM)
    operands = [place, keep, ku, *operators, *own, *far]
    specs = [scalars, scalars, pl.BlockSpec(memory_space=pltpu.VMEM)] + [anywhere] * 9
    aliases = {}
    if previous is not None:
        aliases = {len(operands): 0}
        operands.append(previous)
        specs.append(anywhere)

    def kernel(*refs):
        transform_kernel(index, *refs)

    return pl.pallas_call(
        kernel,
        out_shape=jax.ShapeDtypeStruct((ROWS, PLANES, RUN, 16, 2, G), jnp.bfloat16),
        in_specs=specs,
        out_specs=anywhere,
        input_output_aliases=aliases,
        scratch_shapes=[
            pltpu.VMEM((2, 4, G, G), jnp.bfloat16),
            pltpu.VMEM((PLANES, 2, G, G), jnp.bfloat16),
            pltpu.VMEM((G, G), jnp.bfloat16),
            pltpu.VMEM((G, G), jnp.bfloat16),
            pltpu.VMEM((PLANES, 16 * 64, 2 * G), jnp.bfloat16),
            pltpu.VMEM((PLANES, 16, ROWS, 2, G), jnp.bfloat16),
            pltpu.SemaphoreType.DMA,
            pltpu.SemaphoreType.DMA,
            pltpu.SemaphoreType.DMA,
        ],
        compiler_params=pltpu.CompilerParams(vmem_limit_bytes=40 * 1024 * 1024),
        cost_estimate=pl.CostEstimate(flops=4_300_000_000, bytes_accessed=9_000_000, transcendentals=0),
        name="transform",
    )(*operands)


def gather_operator(w_operator):
    lows, highs = [], []
    for half in range(2):
        held = w_operator[half][None]
        for step in range(3):
            held = jnp.concatenate([held, swap_grid(held, half, step)], 0)
        lows.append(held)
        highs.append(swap_grid(held, half, 3))
    return jnp.stack(lows), highs[0], highs[1]


def select(flags, yes, no):
    return jnp.where(flags[:, None, None, None], yes, no)


def body(jones, owner, mask, w_operator):
    wa = lax.axis_index("wa")
    grid = lax.axis_index("grid")
    core = wa % 2
    slots = owner[:RUN]
    holder = slots // 4
    held = [lax.dynamic_index_in_dim(jones, slots[index] % 4, 0, keepdims=False) for index in range(RUN)]
    mine = jnp.stack([lax.dynamic_index_in_dim(one, core, 1, keepdims=False) for one in held])
    other = jnp.stack([lax.dynamic_index_in_dim(one, 1 - core, 1, keepdims=False) for one in held])
    rows = select(holder % 2 == core, mine, swap_core(other))
    first = jnp.where(core == 0, ZCLASSES[0][0], ZCLASSES[1][0]) // 2
    here = holder // 2 == wa // 2
    rows = select(here, rows, swap_z(rows, 0))
    near = here | (holder // 2 == (wa // 2 ^ first))
    rows = select(near, rows, swap_z(rows, 1))

    operators = gather_operator(w_operator)

    streams = []
    for half in range(2):
        stream = rows[None, :, 2 * half : 2 * half + 2]
        for step in range(2):
            stream = jnp.concatenate([stream, swap_grid(stream, half, step)], 0)
        streams.append((stream, swap_grid(stream, half, 2)))
    masks = jnp.asarray(block_masks())
    own_place = grid ^ lax.dynamic_index_in_dim(masks, core, 0, keepdims=False)
    far_place = grid ^ lax.dynamic_index_in_dim(masks, 1 - core, 0, keepdims=False)
    place = jnp.concatenate([core[None], own_place.reshape(-1), far_place.reshape(-1)]).astype(jnp.int32)
    kr, ki = w_operator[:, 0], w_operator[:, 1]
    plain = jnp.stack([kr, ki], 2).reshape(PLANES, 2 * ROWS, G)
    turned = jnp.stack([-ki, kr], 2).reshape(PLANES, 2 * ROWS, G)
    ku = jnp.concatenate([plain, turned], 1).reshape(PLANES * 4 * ROWS, G)
    keep = mask.reshape(RUN, 16).astype(jnp.float32)

    own, far = [], []
    for index in range(RUN):
        low = jnp.stack([jnp.concatenate([near_[:, index], far_[:, index]], 0) for near_, far_ in streams])
        high = [swap_grid(low[half], half, 3) for half in range(2)]
        own.append((low, *high))
        far.append((swap_core(low), swap_core(high[0]), swap_core(high[1])))
    result = None
    for index in range(RUN):
        result = transform(index, place, keep[index], ku, operators, own[index], far[index], result)
    return result


def solution(mesh):
    return jax.shard_map(
        body,
        mesh=mesh,
        in_specs=(P("wa", None, None, "grid", None), P(), P(), P("wa", None, "grid", None)),
        out_specs=P("grid", "wa", None, None, None, None),
        check_vma=False,
    )
```

```python
import jax
import jax.numpy as jnp
import numpy as np
from jax import lax
from jax.experimental import pallas as pl
from jax.experimental.pallas import tpu as pltpu
from jax.sharding import PartitionSpec as P

RUN = 3
G = 512
ROWS = 32
PLANES = 2

CLASSES = (((1, 3, 4, 12), (3, 4, 12, 1)), ((4, 12, 1, 3), (12, 1, 3, 4)))
ZCLASSES = ((2, 6), (6, 2))

TASKS = (
    ("s", 0, 1),
    ("p", 0, 1),
    ("s", 2, 3),
    ("p", 2, 3),
    ("p", 0, 2),
    ("p", 0, 3),
    ("p", 1, 2),
    ("p", 1, 3),
)


def term(a, b):
    return 8 * (a // 2) + 4 * (b // 2) + 2 * (a % 2) + b % 2


def block_masks():
    table = np.zeros((2, 2, 16), np.int32)
    for core in range(2):
        for half in range(2):
            for block in range(16):
                for step in range(4):
                    if block >> step & 1:
                        table[core, half, block] ^= CLASSES[core][half][step]
    return table


MASKS = block_masks()


def exchange(value, wa_mask, grid_mask):
    perm = []
    for wa in range(8):
        for grid in range(16):
            core = wa % 2
            perm.append((wa * 16 + grid, (wa ^ wa_mask(core)) * 16 + (grid ^ grid_mask(core))))
    return lax.ppermute(value, ("wa", "grid"), perm)


def swap_core(value):
    return exchange(value, lambda core: 1, lambda core: 0)


def swap_z(value, step):
    return exchange(value, lambda core: ZCLASSES[core][step], lambda core: 0)


def swap_grid(value, half, step):
    return exchange(value, lambda core: 0, lambda core: CLASSES[core][half][step])


def pick_kernel(ids, owner, jones, mine, other, semaphore):
    core = ids[0]
    copies = []
    for index in range(RUN):
        slot = owner[index] & 3
        for entry in range(4):
            for part, target in ((core, mine), (1 - core, other)):
                copies.append(
                    pltpu.make_async_copy(
                        jones.at[slot, entry, part], target.at[index, entry], semaphore.at[len(copies)]
                    )
                )
    for copy in copies:
        copy.start()
    for copy in copies:
        copy.wait()


def pick(ids, owner, jones):
    shape = jax.ShapeDtypeStruct((RUN, 4, ROWS, G), jnp.bfloat16)
    scalars = pl.BlockSpec(memory_space=pltpu.SMEM)
    return pl.pallas_call(
        pick_kernel,
        out_shape=(shape, shape),
        in_specs=[scalars, scalars, pl.BlockSpec(memory_space=pl.ANY)],
        out_specs=(pl.BlockSpec(memory_space=pltpu.VMEM), pl.BlockSpec(memory_space=pltpu.VMEM)),
        scratch_shapes=[pltpu.SemaphoreType.DMA((RUN * 8,))],
        compiler_params=pltpu.CompilerParams(vmem_limit_bytes=60 * 1024 * 1024),
        name="pick",
    )(ids, owner, jones)


def transform_kernel(index, *refs):
    ids, keep, ku, k30, k31, k40, k41, own3, own40, own41, far3, far40, far41 = refs[:13]
    out, fields, operator, real0, imag0, real1, imag1, left, staged, sem0, sem1, operator_sem, out_sem = refs[-13:]
    core, grid = ids[0], ids[1]
    own4 = (own40, own41)
    far4 = (far40, far41)
    k3 = (k30, k31)
    k4 = (k40, k41)
    field_sems = (sem0, sem1)
    pairs = ((real0, imag0), (real1, imag1))
    for half in range(2):
        for block in range(16):
            masks = (int(MASKS[0, half, block]), int(MASKS[1, half, block]))
            row = pl.multiple_of((grid ^ jnp.where(core == 0, masks[0], masks[1])) * ROWS, ROWS)
            far_row = pl.multiple_of((grid ^ jnp.where(core == 0, masks[1], masks[0])) * ROWS, ROWS)
            source = own3.at[half, block] if block < 8 else own4[half].at[block - 8]
            pltpu.make_async_copy(
                source, fields.at[half, core, :, pl.ds(row, ROWS)], field_sems[half]
            ).start()
            source = far3.at[half, block] if block < 8 else far4[half].at[block - 8]
            pltpu.make_async_copy(
                source, fields.at[half, 1 - core, :, pl.ds(far_row, ROWS)], field_sems[half]
            ).start()
    for half in range(2):
        for block in range(16):
            masks = (int(MASKS[0, half, block]), int(MASKS[1, half, block]))
            row = pl.multiple_of((grid ^ jnp.where(core == 0, masks[0], masks[1])) * ROWS, ROWS)
            source = k3[half].at[block] if block < 8 else k4[half].at[block - 8]
            pltpu.make_async_copy(source, operator.at[half, :, pl.ds(row, ROWS)], operator_sem).start()

    def products(task, pair):
        kind, a, b = task
        real, imag = pair
        for step in range(G // ROWS):
            rows = slice(step * ROWS, step * ROWS + ROWS)
            ar = fields[a // 2, 0, a % 2, rows].astype(jnp.float32)
            ai = fields[a // 2, 1, a % 2, rows].astype(jnp.float32)
            br = fields[b // 2, 0, b % 2, rows].astype(jnp.float32)
            bi = fields[b // 2, 1, b % 2, rows].astype(jnp.float32)
            if kind == "s":
                real[rows] = (ar * ar + ai * ai).astype(jnp.bfloat16)
                imag[rows] = (br * br + bi * bi).astype(jnp.bfloat16)
            else:
                real[rows] = (ar * br + ai * bi).astype(jnp.bfloat16)
                imag[rows] = (ai * br - ar * bi).astype(jnp.bfloat16)

    def put(plane, entry, columns, value, turned):
        rows = slice(entry * 64, entry * 64 + 64)
        left[plane, rows, columns] = (value * keep[entry]).astype(jnp.bfloat16)
        beside = slice(columns.start + G, columns.stop + G)
        left[plane, rows, beside] = (turned * keep[entry]).astype(jnp.bfloat16)

    def first_pass(task, pair):
        kind, a, b = task
        real, imag = pair
        for start in range(0, G, 256):
            columns = slice(start, start + 256)
            both_a = jnp.dot(ku[...], real[:, columns], preferred_element_type=jnp.float32)
            both_b = jnp.dot(ku[...], imag[:, columns], preferred_element_type=jnp.float32)
            for plane in range(PLANES):
                at = plane * 128
                xa, ya = both_a[at : at + 64], both_a[at + 64 : at + 128]
                xb, yb = both_b[at : at + 64], both_b[at + 64 : at + 128]
                if kind == "s":
                    put(plane, term(a, a), columns, xa, ya)
                    put(plane, term(b, b), columns, xb, yb)
                else:
                    put(plane, term(a, b), columns, xa + yb, ya - xb)
                    put(plane, term(b, a), columns, xa - yb, ya + xb)

    pltpu.make_async_copy(fields.at[0], fields.at[0], sem0).wait()
    products(TASKS[0], pairs[0])
    for step in range(8):
        if step == 1:
            pltpu.make_async_copy(fields.at[1], fields.at[1], sem1).wait()
        if step < 7:
            products(TASKS[step + 1], pairs[(step + 1) % 2])
        first_pass(TASKS[step], pairs[step % 2])

    pltpu.make_async_copy(operator, operator, operator_sem).wait()
    contract = (((1,), (1,)), ((), ()))
    for plane in range(PLANES):
        for group in range(4):
            rows = slice(group * 256, group * 256 + 256)
            total = lax.dot_general(
                left[plane, rows, 0:G], operator[plane, 0], contract, preferred_element_type=jnp.float32
            ) + lax.dot_general(
                left[plane, rows, G : 2 * G], operator[plane, 1], contract, preferred_element_type=jnp.float32
            )
            staged[plane, group * 4 : group * 4 + 4] = total.astype(jnp.bfloat16).reshape(4, ROWS, 2, G)
            for entry in range(group * 4, group * 4 + 4):
                pltpu.make_async_copy(
                    staged.at[plane, entry], out.at[:, plane, index, entry], out_sem
                ).start()
    pltpu.make_async_copy(staged, staged, out_sem).wait()


def transform(index, ids, keep, ku, operators, own, far, previous):
    anywhere = pl.BlockSpec(memory_space=pl.ANY)
    scalars = pl.BlockSpec(memory_space=pltpu.SMEM)
    operands = [ids, keep, ku, *operators, *own, *far]
    specs = [scalars, scalars, pl.BlockSpec(memory_space=pltpu.VMEM)] + [anywhere] * 10
    aliases = {}
    if previous is not None:
        aliases = {len(operands): 0}
        operands.append(previous)
        specs.append(anywhere)

    def kernel(*refs):
        transform_kernel(index, *refs)

    return pl.pallas_call(
        kernel,
        out_shape=jax.ShapeDtypeStruct((ROWS, PLANES, RUN, 16, 2, G), jnp.bfloat16),
        in_specs=specs,
        out_specs=anywhere,
        input_output_aliases=aliases,
        scratch_shapes=[
            pltpu.VMEM((2, 2, 2, G, G), jnp.bfloat16),
            pltpu.VMEM((PLANES, 2, G, G), jnp.bfloat16),
            pltpu.VMEM((G, G), jnp.bfloat16),
            pltpu.VMEM((G, G), jnp.bfloat16),
            pltpu.VMEM((G, G), jnp.bfloat16),
            pltpu.VMEM((G, G), jnp.bfloat16),
            pltpu.VMEM((PLANES, 16 * 64, 2 * G), jnp.bfloat16),
            pltpu.VMEM((PLANES, 16, ROWS, 2, G), jnp.bfloat16),
            pltpu.SemaphoreType.DMA,
            pltpu.SemaphoreType.DMA,
            pltpu.SemaphoreType.DMA,
            pltpu.SemaphoreType.DMA,
        ],
        compiler_params=pltpu.CompilerParams(vmem_limit_bytes=24 * 1024 * 1024),
        cost_estimate=pl.CostEstimate(flops=1_000_000, bytes_accessed=1_000_000, transcendentals=0),
        name="transform",
    )(*operands)


def after(value, *others):
    return lax.optimization_barrier((value, *others))[0]


def choose(flags, yes, no):
    return jnp.where(flags[:, None, None, None], yes, no)


def body(jones, owner, mask, w_operator):
    wa = lax.axis_index("wa")
    grid = lax.axis_index("grid")
    core = wa & 1
    ids = jnp.stack([core, grid]).astype(jnp.int32)
    mine, other = pick(ids, owner, jones)

    planes = [w_operator[half][None] for half in range(2)]
    planes = [jnp.concatenate([planes[half], swap_grid(planes[half], half, 0)], 0) for half in range(2)]

    holder = owner[:RUN] >> 2
    rows = choose((holder & 1) == core, mine, swap_core(other))
    first = ZCLASSES[0][0] + core * (ZCLASSES[1][0] - ZCLASSES[0][0])
    apart = (holder ^ wa) & 6
    rows = after(rows, *planes)
    planes = [jnp.concatenate([planes[half], swap_grid(planes[half], half, 1)], 0) for half in range(2)]
    rows = choose(apart == 0, rows, swap_z(rows, 0))
    rows = after(rows, *planes)
    planes = [jnp.concatenate([planes[half], swap_grid(planes[half], half, 2)], 0) for half in range(2)]
    rows = choose((apart == 0) | (apart == first), rows, swap_z(rows, 1))
    rows = after(rows, *planes)
    last_planes = [swap_grid(planes[half], half, 3) for half in range(2)]
    operators = (*planes, *last_planes)

    streams = []
    for half in range(2):
        stream = rows[None, :, 2 * half : 2 * half + 2]
        stream = jnp.concatenate([stream, swap_grid(stream, half, 0)], 0)
        stream = jnp.concatenate([stream, swap_grid(stream, half, 1)], 0)
        stream = after(stream, *last_planes)
        streams.append((stream, swap_grid(stream, half, 2)))

    kr, ki = w_operator[:, 0], w_operator[:, 1]
    plain = jnp.stack([kr, ki], 2).reshape(PLANES, 2 * ROWS, G)
    turned = jnp.stack([-ki, kr], 2).reshape(PLANES, 2 * ROWS, G)
    ku = jnp.concatenate([plain, turned], 1).reshape(PLANES * 4 * ROWS, G)
    keep = mask.reshape(RUN, 16).astype(jnp.float32)

    lows = []
    highs = []
    for index in range(RUN):
        low = jnp.stack([jnp.concatenate([near[:, index], far[:, index]], 0) for near, far in streams])
        send = [low[half] for half in range(2)]
        if index == 2:
            send = [after(send[half], highs[0][half]) for half in range(2)]
        lows.append(low)
        highs.append([swap_grid(send[half], half, 3) for half in range(2)])
    result = None
    for index in range(RUN):
        own = (lows[index], *highs[index])
        sent = highs[index]
        if result is not None:
            sent = [after(one, result) for one in sent]
        far = (swap_core(lows[index]), *[swap_core(one) for one in sent])
        result = transform(index, ids, keep[index], ku, operators, own, far, result)
    return result


def solution(mesh):
    return jax.shard_map(
        body,
        mesh=mesh,
        in_specs=(P("wa", None, None, "grid", None), P(), P(), P("wa", None, "grid", None)),
        out_specs=P("grid", "wa", None, None, None, None),
        check_vma=False,
    )
```

```python
import jax
import jax.numpy as jnp
import numpy as np
from jax import lax
from jax.experimental import pallas as pl
from jax.experimental.pallas import tpu as pltpu
from jax.sharding import PartitionSpec as P

RUN = 3
G = 512
ROWS = 32
PLANES = 2

CLASSES = (((1, 3, 4, 12), (3, 4, 12, 1)), ((4, 12, 1, 3), (12, 1, 3, 4)))
ZCLASSES = ((2, 6), (6, 2))

PAIRS = ((0, 1), (0, 2), (0, 3), (1, 2), (1, 3), (2, 3))


def term(a, b):
    return 8 * (a // 2) + 4 * (b // 2) + 2 * (a % 2) + b % 2


def block_masks():
    table = np.zeros((2, 2, 16), np.int32)
    for core in range(2):
        for half in range(2):
            for block in range(16):
                for step in range(4):
                    if block >> step & 1:
                        table[core, half, block] ^= CLASSES[core][half][step]
    return table


MASKS = block_masks()


def exchange(value, wa_mask, grid_mask):
    perm = []
    for wa in range(8):
        for grid in range(16):
            core = wa % 2
            perm.append((wa * 16 + grid, (wa ^ wa_mask(core)) * 16 + (grid ^ grid_mask(core))))
    return lax.ppermute(value, ("wa", "grid"), perm)


def swap_core(value):
    return exchange(value, lambda core: 1, lambda core: 0)


def swap_z(value, step):
    return exchange(value, lambda core: ZCLASSES[core][step], lambda core: 0)


def swap_grid(value, half, step):
    return exchange(value, lambda core: 0, lambda core: CLASSES[core][half][step])


def pick_kernel(ids, owner, jones, mine, other, semaphore):
    core = ids[0]
    copies = []
    for index in range(RUN):
        slot = owner[index] & 3
        for entry in range(4):
            for part, target in ((core, mine), (1 - core, other)):
                copies.append(
                    pltpu.make_async_copy(
                        jones.at[slot, entry, part], target.at[index, entry], semaphore.at[len(copies)]
                    )
                )
    for copy in copies:
        copy.start()
    for copy in copies:
        copy.wait()


def pick(ids, owner, jones):
    shape = jax.ShapeDtypeStruct((RUN, 4, ROWS, G), jnp.bfloat16)
    scalars = pl.BlockSpec(memory_space=pltpu.SMEM)
    return pl.pallas_call(
        pick_kernel,
        out_shape=(shape, shape),
        in_specs=[scalars, scalars, pl.BlockSpec(memory_space=pl.ANY)],
        out_specs=(pl.BlockSpec(memory_space=pltpu.VMEM), pl.BlockSpec(memory_space=pltpu.VMEM)),
        scratch_shapes=[pltpu.SemaphoreType.DMA((RUN * 8,))],
        compiler_params=pltpu.CompilerParams(vmem_limit_bytes=60 * 1024 * 1024),
        name="pick",
    )(ids, owner, jones)


def transform_kernel(index, *refs):
    ids, keep, ku = refs[:3]
    gathered = refs[3:5]
    own = (refs[5:7], refs[7:9])
    far = (refs[9:11], refs[11:13])
    out, fields, operator, products, left, staged, field_sem, operator_sem, out_sem = refs[-9:]
    core, grid = ids[0], ids[1]

    def placed(half, block, near):
        masks = (int(MASKS[0, half, block]), int(MASKS[1, half, block]))
        chosen = jnp.where(core == 0, masks[0], masks[1]) if near else jnp.where(core == 0, masks[1], masks[0])
        return pl.ds(pl.multiple_of((grid ^ chosen) * ROWS, ROWS), ROWS)

    for half in range(2):
        for block in range(16):
            for near, source, part in ((True, own, core), (False, far, 1 - core)):
                pltpu.make_async_copy(
                    source[block // 8][half].at[block % 8],
                    fields.at[part, pl.ds(2 * half, 2), placed(half, block, near)],
                    field_sem,
                ).start()
    for block in range(16):
        pltpu.make_async_copy(
            gathered[block // 8].at[block % 8], operator.at[:, :, placed(0, block, True)], operator_sem
        ).start()

    def multiply(columns):
        for start in range(0, G, 16):
            rows = slice(start, start + 16)
            re = [fields[0, entry, rows, columns].astype(jnp.float32) for entry in range(4)]
            im = [fields[1, entry, rows, columns].astype(jnp.float32) for entry in range(4)]
            for a in range(4):
                products[a, rows, columns] = (re[a] * re[a] + im[a] * im[a]).astype(jnp.bfloat16)
            for at, (a, b) in enumerate(PAIRS):
                products[4 + 2 * at, rows, columns] = (re[a] * re[b] + im[a] * im[b]).astype(jnp.bfloat16)
                products[5 + 2 * at, rows, columns] = (im[a] * re[b] - re[a] * im[b]).astype(jnp.bfloat16)

    def put(plane, entry, columns, value, turned):
        rows = slice(entry * 64, entry * 64 + 64)
        left[plane, rows, columns] = value.astype(jnp.bfloat16)
        left[plane, rows, slice(columns.start + G, columns.stop + G)] = turned.astype(jnp.bfloat16)

    def first_pass(columns):
        def apply(field):
            return jnp.dot(ku[...], products[field, :, columns], preferred_element_type=jnp.float32)

        for a in range(4):
            whole = apply(a)
            for plane in range(PLANES):
                at = plane * 128
                put(plane, term(a, a), columns, whole[at : at + 64], whole[at + 64 : at + 128])
        for pair, (a, b) in enumerate(PAIRS):
            real, imag = apply(4 + 2 * pair), apply(5 + 2 * pair)
            for plane in range(PLANES):
                at = plane * 128
                xa, ya = real[at : at + 64], real[at + 64 : at + 128]
                xb, yb = imag[at : at + 64], imag[at + 64 : at + 128]
                put(plane, term(a, b), columns, xa + yb, ya - xb)
                put(plane, term(b, a), columns, xa - yb, ya + xb)

    chunks = [slice(start, start + 256) for start in range(0, G, 256)]
    pltpu.make_async_copy(fields, fields, field_sem).wait()
    multiply(chunks[0])
    for step, chunk in enumerate(chunks):
        if step + 1 < len(chunks):
            multiply(chunks[step + 1])
        first_pass(chunk)
    for entry in range(16):

        @pl.when(keep[entry] == 0)
        def _(entry=entry):
            left[:, entry * 64 : entry * 64 + 64] = jnp.zeros((PLANES, 64, 2 * G), jnp.bfloat16)

    pltpu.make_async_copy(operator, operator, operator_sem).wait()
    contract = (((1,), (1,)), ((), ()))
    for plane in range(PLANES):
        for group in range(4):
            rows = slice(group * 256, group * 256 + 256)
            total = lax.dot_general(
                left[plane, rows, 0:G], operator[plane, 0], contract, preferred_element_type=jnp.float32
            ) + lax.dot_general(
                left[plane, rows, G : 2 * G], operator[plane, 1], contract, preferred_element_type=jnp.float32
            )
            staged[plane, group * 4 : group * 4 + 4] = total.astype(jnp.bfloat16).reshape(4, ROWS, 2, G)
            for entry in range(group * 4, group * 4 + 4):
                pltpu.make_async_copy(
                    staged.at[plane, entry], out.at[:, plane, index, entry], out_sem
                ).start()
    pltpu.make_async_copy(staged, staged, out_sem).wait()


def transform(index, ids, keep, ku, operators, own, far, previous):
    anywhere = pl.BlockSpec(memory_space=pl.ANY)
    scalars = pl.BlockSpec(memory_space=pltpu.SMEM)
    operands = [ids, keep, ku, *operators, *own, *far]
    specs = [scalars, scalars, pl.BlockSpec(memory_space=pltpu.VMEM)] + [anywhere] * 10
    aliases = {}
    if previous is not None:
        aliases = {len(operands): 0}
        operands.append(previous)
        specs.append(anywhere)

    def kernel(*refs):
        transform_kernel(index, *refs)

    return pl.pallas_call(
        kernel,
        out_shape=jax.ShapeDtypeStruct((ROWS, PLANES, RUN, 16, 2, G), jnp.bfloat16),
        in_specs=specs,
        out_specs=anywhere,
        input_output_aliases=aliases,
        scratch_shapes=[
            pltpu.VMEM((2, 4, G, G), jnp.bfloat16),
            pltpu.VMEM((PLANES, 2, G, G), jnp.bfloat16),
            pltpu.VMEM((16, G, G), jnp.bfloat16),
            pltpu.VMEM((PLANES, 16 * 64, 2 * G), jnp.bfloat16),
            pltpu.VMEM((PLANES, 16, ROWS, 2, G), jnp.bfloat16),
            pltpu.SemaphoreType.DMA,
            pltpu.SemaphoreType.DMA,
            pltpu.SemaphoreType.DMA,
        ],
        compiler_params=pltpu.CompilerParams(vmem_limit_bytes=26 * 1024 * 1024),
        cost_estimate=pl.CostEstimate(flops=1_000_000, bytes_accessed=1_000_000, transcendentals=0),
        name="transform",
    )(*operands)


def after(value, *others):
    return lax.optimization_barrier((value, *others))[0]


def choose(flags, yes, no):
    return jnp.where(flags[:, None, None, None], yes, no)


def body(jones, owner, mask, w_operator):
    wa = lax.axis_index("wa")
    grid = lax.axis_index("grid")
    core = wa & 1
    ids = jnp.stack([core, grid]).astype(jnp.int32)
    mine, other = pick(ids, owner, jones)

    blocks = w_operator[None]
    blocks = jnp.concatenate([blocks, swap_grid(blocks, 0, 0)], 0)

    holder = owner[:RUN] >> 2
    rows = choose((holder & 1) == core, mine, swap_core(other))
    first = ZCLASSES[0][0] + core * (ZCLASSES[1][0] - ZCLASSES[0][0])
    apart = (holder ^ wa) & 6
    rows = after(rows, blocks)
    blocks = jnp.concatenate([blocks, swap_grid(blocks, 0, 1)], 0)
    rows = choose(apart == 0, rows, swap_z(rows, 0))
    rows = after(rows, blocks)
    blocks = jnp.concatenate([blocks, swap_grid(blocks, 0, 2)], 0)
    rows = choose((apart == 0) | (apart == first), rows, swap_z(rows, 1))
    rows = after(rows, blocks)
    operators = (blocks, swap_grid(blocks, 0, 3))

    streams = []
    for half in range(2):
        stream = rows[None, :, 2 * half : 2 * half + 2]
        for step in range(2):
            stream = jnp.concatenate([stream, swap_grid(stream, half, step)], 0)
        stream = after(stream, *operators)
        streams.append((stream, swap_grid(stream, half, 2)))

    kr, ki = w_operator[:, 0], w_operator[:, 1]
    plain = jnp.stack([kr, ki], 2).reshape(PLANES, 2 * ROWS, G)
    turned = jnp.stack([-ki, kr], 2).reshape(PLANES, 2 * ROWS, G)
    ku = jnp.concatenate([plain, turned], 1).reshape(PLANES * 4 * ROWS, G)
    keep = mask.reshape(RUN, 16)

    own = []
    for index in range(RUN):
        low = [jnp.concatenate([near[:, index], far[:, index]], 0) for near, far in streams]
        send = low
        if index == 2:
            send = [after(send[half], own[0][2 + half]) for half in range(2)]
        own.append((*low, *[swap_grid(send[half], half, 3) for half in range(2)]))
    result = None
    for index in range(RUN):
        sent = own[index]
        if result is not None:
            sent = [*sent[:2], *[after(one, result) for one in sent[2:]]]
        far = [swap_core(one) for one in sent]
        result = transform(index, ids, keep[index], ku, operators, own[index], far, result)
    return result


def solution(mesh):
    return jax.shard_map(
        body,
        mesh=mesh,
        in_specs=(P("wa", None, None, "grid", None), P(), P(), P("wa", None, "grid", None)),
        out_specs=P("grid", "wa", None, None, None, None),
        check_vma=False,
    )
```

```python
import jax
import jax.numpy as jnp
import numpy as np
from jax import lax
from jax.experimental import pallas as pl
from jax.experimental.pallas import tpu as pltpu
from jax.sharding import PartitionSpec as P

RUN = 3
G = 512
ROWS = 32
PLANES = 2

CLASSES = (((1, 3, 4, 12), (3, 4, 12, 1)), ((4, 12, 1, 3), (12, 1, 3, 4)))
ZCLASSES = ((2, 6), (6, 2))

MEMBERS = (0, 2, 3)

PAIRS = ((0, 1), (0, 2), (0, 3), (1, 2), (1, 3), (2, 3))


def term(a, b):
    return 8 * (a // 2) + 4 * (b // 2) + 2 * (a % 2) + b % 2


def block_masks():
    table = np.zeros((2, 2, 16), np.int32)
    for core in range(2):
        for half in range(2):
            for block in range(16):
                for step in range(4):
                    if block >> step & 1:
                        table[core, half, block] ^= CLASSES[core][half][step]
    return table


MASKS = block_masks()


def exchange(value, wa_mask, grid_mask):
    perm = []
    for wa in range(8):
        for grid in range(16):
            core = wa % 2
            perm.append((wa * 16 + grid, (wa ^ wa_mask(core)) * 16 + (grid ^ grid_mask(core))))
    return lax.ppermute(value, ("wa", "grid"), perm)


def swap_core(value):
    return exchange(value, lambda core: 1, lambda core: 0)


def swap_z(value, step):
    return exchange(value, lambda core: ZCLASSES[core][step], lambda core: 0)


def swap_grid(value, half, step):
    return exchange(value, lambda core: 0, lambda core: CLASSES[core][half][step])


def pick_kernel(ids, owner, jones, mine, other, semaphore):
    core = ids[0]
    copies = []
    for index in range(RUN):
        slot = owner[index] & 3
        for part, target in ((core, mine), (1 - core, other)):
            copies.append(
                pltpu.make_async_copy(jones.at[slot, :, part], target.at[index], semaphore.at[len(copies)])
            )
    for copy in copies:
        copy.start()
    for copy in copies:
        copy.wait()


def pick(ids, owner, jones):
    shape = jax.ShapeDtypeStruct((RUN, 4, ROWS, G), jnp.bfloat16)
    scalars = pl.BlockSpec(memory_space=pltpu.SMEM)
    return pl.pallas_call(
        pick_kernel,
        out_shape=(shape, shape),
        in_specs=[scalars, scalars, pl.BlockSpec(memory_space=pl.ANY)],
        out_specs=(pl.BlockSpec(memory_space=pltpu.VMEM), pl.BlockSpec(memory_space=pltpu.VMEM)),
        scratch_shapes=[pltpu.SemaphoreType.DMA((RUN * 2,))],
        compiler_params=pltpu.CompilerParams(vmem_limit_bytes=60 * 1024 * 1024),
        name="pick",
    )(ids, owner, jones)


def transform_kernel(index, *refs):
    ids, keep, ku = refs[:3]
    own = (refs[3:5], refs[5:7], refs[7:9])
    far = (refs[9:11], refs[11:13], refs[13:15])
    lasts = refs[15:17]
    member = MEMBERS[index]
    out, fields, operator, products, left, staged, field_sem, operator_sem, out_sem = refs[-9:]
    core, grid = ids[0], ids[1]

    def placed(half, block, near):
        masks = (int(MASKS[0, half, block]), int(MASKS[1, half, block]))
        chosen = jnp.where(core == 0, masks[0], masks[1]) if near else jnp.where(core == 0, masks[1], masks[0])
        return pl.ds(pl.multiple_of((grid ^ chosen) * ROWS, ROWS), ROWS)

    def block_of(group, half, block, at):
        if block < 8:
            return group[block // 4][half].at[block % 4, at]
        return group[2][half].at[block - 8, 0]

    for half in range(2):
        for block in range(16):
            for near, source, part in ((True, own, core), (False, far, 1 - core)):
                pltpu.make_async_copy(
                    block_of(source, half, block, member),
                    fields.at[part, pl.ds(2 * half, 2), placed(half, block, near)],
                    field_sem,
                ).start()
    for half in range(2):
        for block in range(16):
            source = block_of(own, half, block, 1) if block < 8 else lasts[half].at[block - 8, 1]
            pltpu.make_async_copy(source, operator.at[half, :, placed(half, block, True)], operator_sem).start()

    def multiply(columns):
        for start in range(0, G, 16):
            rows = slice(start, start + 16)
            re = [fields[0, entry, rows, columns].astype(jnp.float32) for entry in range(4)]
            im = [fields[1, entry, rows, columns].astype(jnp.float32) for entry in range(4)]
            for a in range(4):
                products[a, rows, columns] = (re[a] * re[a] + im[a] * im[a]).astype(jnp.bfloat16)
            for at, (a, b) in enumerate(PAIRS):
                products[4 + 2 * at, rows, columns] = (re[a] * re[b] + im[a] * im[b]).astype(jnp.bfloat16)
                products[5 + 2 * at, rows, columns] = (im[a] * re[b] - re[a] * im[b]).astype(jnp.bfloat16)

    def put(plane, entry, columns, value, turned):
        rows = slice(entry * 64, entry * 64 + 64)
        left[plane, rows, columns] = value.astype(jnp.bfloat16)
        left[plane, rows, slice(columns.start + G, columns.stop + G)] = turned.astype(jnp.bfloat16)

    def first_pass(columns):
        def apply(field):
            return jnp.dot(ku[...], products[field, :, columns], preferred_element_type=jnp.float32)

        for a in range(4):
            whole = apply(a)
            for plane in range(PLANES):
                at = plane * 128
                put(plane, term(a, a), columns, whole[at : at + 64], whole[at + 64 : at + 128])
        for pair, (a, b) in enumerate(PAIRS):
            real, imag = apply(4 + 2 * pair), apply(5 + 2 * pair)
            for plane in range(PLANES):
                at = plane * 128
                xa, ya = real[at : at + 64], real[at + 64 : at + 128]
                xb, yb = imag[at : at + 64], imag[at + 64 : at + 128]
                put(plane, term(a, b), columns, xa + yb, ya - xb)
                put(plane, term(b, a), columns, xa - yb, ya + xb)

    chunks = [slice(start, start + 256) for start in range(0, G, 256)]
    pltpu.make_async_copy(fields, fields, field_sem).wait()
    multiply(chunks[0])
    for step, chunk in enumerate(chunks):
        if step + 1 < len(chunks):
            multiply(chunks[step + 1])
        first_pass(chunk)
    for entry in range(16):

        @pl.when(keep[entry] == 0)
        def _(entry=entry):
            left[:, entry * 64 : entry * 64 + 64] = jnp.zeros((PLANES, 64, 2 * G), jnp.bfloat16)

    pltpu.make_async_copy(operator, operator, operator_sem).wait()
    contract = (((1,), (1,)), ((), ()))
    for plane in range(PLANES):
        for group in range(4):
            rows = slice(group * 256, group * 256 + 256)
            total = lax.dot_general(
                left[plane, rows, 0:G], operator[plane, 0], contract, preferred_element_type=jnp.float32
            ) + lax.dot_general(
                left[plane, rows, G : 2 * G], operator[plane, 1], contract, preferred_element_type=jnp.float32
            )
            staged[plane, group * 4 : group * 4 + 4] = total.astype(jnp.bfloat16).reshape(4, ROWS, 2, G)
            for entry in range(group * 4, group * 4 + 4):
                pltpu.make_async_copy(
                    staged.at[plane, entry], out.at[:, plane, index, entry], out_sem
                ).start()
    pltpu.make_async_copy(staged, staged, out_sem).wait()


def transform(index, ids, keep, ku, own, far, lasts, previous):
    anywhere = pl.BlockSpec(memory_space=pl.ANY)
    scalars = pl.BlockSpec(memory_space=pltpu.SMEM)
    operands = [ids, keep, ku, *own, *far, *lasts]
    specs = [scalars, scalars, pl.BlockSpec(memory_space=pltpu.VMEM)] + [anywhere] * 14
    aliases = {}
    if previous is not None:
        aliases = {len(operands): 0}
        operands.append(previous)
        specs.append(anywhere)

    def kernel(*refs):
        transform_kernel(index, *refs)

    return pl.pallas_call(
        kernel,
        out_shape=jax.ShapeDtypeStruct((ROWS, PLANES, RUN, 16, 2, G), jnp.bfloat16),
        in_specs=specs,
        out_specs=anywhere,
        input_output_aliases=aliases,
        scratch_shapes=[
            pltpu.VMEM((2, 4, G, G), jnp.bfloat16),
            pltpu.VMEM((PLANES, 2, G, G), jnp.bfloat16),
            pltpu.VMEM((16, G, G), jnp.bfloat16),
            pltpu.VMEM((PLANES, 16 * 64, 2 * G), jnp.bfloat16),
            pltpu.VMEM((PLANES, 16, ROWS, 2, G), jnp.bfloat16),
            pltpu.SemaphoreType.DMA,
            pltpu.SemaphoreType.DMA,
            pltpu.SemaphoreType.DMA,
        ],
        compiler_params=pltpu.CompilerParams(vmem_limit_bytes=26 * 1024 * 1024),
        cost_estimate=pl.CostEstimate(flops=1_000_000, bytes_accessed=1_000_000, transcendentals=0),
        name="transform",
    )(*operands)


def after(value, *others):
    return lax.optimization_barrier((value, *others))[0]


def choose(flags, yes, no):
    return jnp.where(flags[:, None, None, None], yes, no)


def body(jones, owner, mask, w_operator):
    wa = lax.axis_index("wa")
    grid = lax.axis_index("grid")
    core = wa & 1
    ids = jnp.stack([core, grid]).astype(jnp.int32)
    mine, other = pick(ids, owner, jones)

    holder = owner[:RUN] >> 2
    rows = choose((holder & 1) == core, mine, swap_core(other))
    first = ZCLASSES[0][0] + core * (ZCLASSES[1][0] - ZCLASSES[0][0])
    apart = (holder ^ wa) & 6
    rows = choose(apart == 0, rows, swap_z(rows, 0))
    rows = choose((apart == 0) | (apart == first), rows, swap_z(rows, 1))

    near, next_blocks = [], []
    for half in range(2):
        of_types = rows[:, 2 * half : 2 * half + 2]
        stream = jnp.concatenate([of_types[:1], w_operator[half : half + 1], of_types[1:]], 0)[None]
        for step in range(2):
            stream = jnp.concatenate([stream, swap_grid(stream, half, step)], 0)
        near.append(stream)
        next_blocks.append(swap_grid(stream, half, 2))
    far_near = [swap_core(one) for one in near]
    far_next = [swap_core(one) for one in next_blocks]

    kr, ki = w_operator[:, 0], w_operator[:, 1]
    plain = jnp.stack([kr, ki], 2).reshape(PLANES, 2 * ROWS, G)
    turned = jnp.stack([-ki, kr], 2).reshape(PLANES, 2 * ROWS, G)
    ku = jnp.concatenate([plain, turned], 1).reshape(PLANES * 4 * ROWS, G)
    keep = mask.reshape(RUN, 16)

    lasts = []
    for index in range(RUN):
        members = slice(0, 2) if index == 0 else slice(MEMBERS[index], MEMBERS[index] + 1)
        send = [jnp.concatenate([near[half][:, members], next_blocks[half][:, members]], 0) for half in range(2)]
        if index == 2:
            send = [after(send[half], lasts[0][half]) for half in range(2)]
        lasts.append([swap_grid(send[half], half, 3) for half in range(2)])
    result = None
    for index in range(RUN):
        sent = [last[:, :1] for last in lasts[index]]
        if result is not None:
            sent = [after(one, result) for one in sent]
        far_last = [swap_core(one) for one in sent]
        own = (*near, *next_blocks, *lasts[index])
        far = (*far_near, *far_next, *far_last)
        result = transform(index, ids, keep[index], ku, own, far, lasts[0], result)
    return result


def solution(mesh):
    return jax.shard_map(
        body,
        mesh=mesh,
        in_specs=(P("wa", None, None, "grid", None), P(), P(), P("wa", None, "grid", None)),
        out_specs=P("grid", "wa", None, None, None, None),
        check_vma=False,
    )
```

```python
import jax
import jax.numpy as jnp
import numpy as np
from jax import lax
from jax.experimental import pallas as pl
from jax.experimental.pallas import tpu as pltpu
from jax.sharding import PartitionSpec as P

RUN = 3
G = 512
ROWS = 32
PLANES = 2

CLASSES = (((1, 3, 4, 12), (1, 3, 12, 4)), ((4, 12, 1, 3), (4, 12, 3, 1)))
ZCLASSES = ((2, 6), (6, 2))

MEMBERS = (0, 2, 3)

PAIRS = ((0, 1), (0, 2), (0, 3), (1, 2), (1, 3), (2, 3))


def term(a, b):
    return 8 * (a // 2) + 4 * (b // 2) + 2 * (a % 2) + b % 2


def block_masks():
    table = np.zeros((2, 2, 16), np.int32)
    for core in range(2):
        for half in range(2):
            for block in range(16):
                for step in range(4):
                    if block >> step & 1:
                        table[core, half, block] ^= CLASSES[core][half][step]
    return table


MASKS = block_masks()


def exchange(value, wa_mask, grid_mask):
    perm = []
    for wa in range(8):
        for grid in range(16):
            core = wa % 2
            perm.append((wa * 16 + grid, (wa ^ wa_mask(core)) * 16 + (grid ^ grid_mask(core))))
    return lax.ppermute(value, ("wa", "grid"), perm)


def swap_core(value):
    return exchange(value, lambda core: 1, lambda core: 0)


def swap_z(value, step):
    return exchange(value, lambda core: ZCLASSES[core][step], lambda core: 0)


def swap_grid(value, half, step):
    return exchange(value, lambda core: 0, lambda core: CLASSES[core][half][step])


def swap_ring(value, turn):
    masks = [(one[0][0], one[0][1], one[0][0] ^ one[0][1])[turn] for one in CLASSES]
    return exchange(value, lambda core: 0, lambda core: masks[core])


def pick_kernel(ids, owner, jones, mine, other, semaphore):
    core = ids[0]
    copies = []
    for index in range(RUN):
        slot = owner[index] & 3
        for part, target in ((core, mine), (1 - core, other)):
            copies.append(
                pltpu.make_async_copy(jones.at[slot, :, part], target.at[index], semaphore.at[len(copies)])
            )
    for copy in copies:
        copy.start()
    for copy in copies:
        copy.wait()


def pick(ids, owner, jones):
    shape = jax.ShapeDtypeStruct((RUN, 4, ROWS, G), jnp.bfloat16)
    scalars = pl.BlockSpec(memory_space=pltpu.SMEM)
    return pl.pallas_call(
        pick_kernel,
        out_shape=(shape, shape),
        in_specs=[scalars, scalars, pl.BlockSpec(memory_space=pl.ANY)],
        out_specs=(pl.BlockSpec(memory_space=pltpu.VMEM), pl.BlockSpec(memory_space=pltpu.VMEM)),
        scratch_shapes=[pltpu.SemaphoreType.DMA((RUN * 2,))],
        compiler_params=pltpu.CompilerParams(vmem_limit_bytes=60 * 1024 * 1024),
        name="pick",
    )(ids, owner, jones)


def transform_kernel(types, *refs):
    ids, keep, ku = refs[:3]
    own = (refs[3:5], refs[5:7], refs[11:13])
    far = (refs[7:9], refs[9:11], refs[13:15])
    lasts = refs[15:17] if len(types) > 1 else refs[11:13]
    out, fields, operator, products, left, staged, field_sems, operator_sem, out_sems = refs[-9:]
    core, grid = ids[0], ids[1]

    def placed(half, block, near):
        masks = (int(MASKS[0, half, block]), int(MASKS[1, half, block]))
        chosen = jnp.where(core == 0, masks[0], masks[1]) if near else jnp.where(core == 0, masks[1], masks[0])
        return pl.ds(pl.multiple_of((grid ^ chosen) * ROWS, ROWS), ROWS)

    def block_of(group, half, block, member, last_member):
        if block < 8:
            return group[block // 4][half].at[block % 4, member]
        return group[2][half].at[block - 8, last_member]

    def load(turn):
        for half in range(2):
            for block in range(16):
                for near, source, part in ((True, own, core), (False, far, 1 - core)):
                    pltpu.make_async_copy(
                        block_of(source, half, block, MEMBERS[types[turn]], turn),
                        fields.at[turn, part, pl.ds(2 * half, 2), placed(half, block, near)],
                        field_sems.at[turn],
                    ).start()

    load(0)
    for half in range(2):
        for block in range(16):
            source = block_of(own, half, block, 1, 0) if block < 8 else lasts[half].at[block - 8, 1]
            pltpu.make_async_copy(source, operator.at[half, :, placed(half, block, True)], operator_sem).start()
    for turn in range(1, len(types)):
        load(turn)

    def multiply(turn, columns):
        for start in range(0, G, 16):
            rows = slice(start, start + 16)
            re = [fields[turn, 0, entry, rows, columns].astype(jnp.float32) for entry in range(4)]
            im = [fields[turn, 1, entry, rows, columns].astype(jnp.float32) for entry in range(4)]
            for a in range(4):
                products[a, rows, columns] = (re[a] * re[a] + im[a] * im[a]).astype(jnp.bfloat16)
            for at, (a, b) in enumerate(PAIRS):
                products[4 + 2 * at, rows, columns] = (re[a] * re[b] + im[a] * im[b]).astype(jnp.bfloat16)
                products[5 + 2 * at, rows, columns] = (im[a] * re[b] - re[a] * im[b]).astype(jnp.bfloat16)

    def put(plane, entry, columns, value, turned):
        rows = slice(entry * 64, entry * 64 + 64)
        left[plane, rows, columns] = value.astype(jnp.bfloat16)
        left[plane, rows, slice(columns.start + G, columns.stop + G)] = turned.astype(jnp.bfloat16)

    def first_pass(columns):
        def apply(field):
            return jnp.dot(ku[...], products[field, :, columns], preferred_element_type=jnp.float32)

        for a in range(4):
            whole = apply(a)
            for plane in range(PLANES):
                at = plane * 128
                put(plane, term(a, a), columns, whole[at : at + 64], whole[at + 64 : at + 128])
        for pair, (a, b) in enumerate(PAIRS):
            real, imag = apply(4 + 2 * pair), apply(5 + 2 * pair)
            for plane in range(PLANES):
                at = plane * 128
                xa, ya = real[at : at + 64], real[at + 64 : at + 128]
                xb, yb = imag[at : at + 64], imag[at + 64 : at + 128]
                put(plane, term(a, b), columns, xa + yb, ya - xb)
                put(plane, term(b, a), columns, xa - yb, ya + xb)

    chunks = [slice(start, start + 256) for start in range(0, G, 256)]
    contract = (((1,), (1,)), ((), ()))
    for turn, index in enumerate(types):
        pltpu.make_async_copy(fields.at[turn], fields.at[turn], field_sems.at[turn]).wait()
        multiply(turn, chunks[0])
        for step, chunk in enumerate(chunks):
            if step + 1 < len(chunks):
                multiply(turn, chunks[step + 1])
            first_pass(chunk)
        for entry in range(16):

            @pl.when(keep[index * 16 + entry] == 0)
            def _(entry=entry):
                left[:, entry * 64 : entry * 64 + 64] = jnp.zeros((PLANES, 64, 2 * G), jnp.bfloat16)

        if turn == 0:
            pltpu.make_async_copy(operator, operator, operator_sem).wait()
        for plane in range(PLANES):
            for group in range(4):
                rows = slice(group * 256, group * 256 + 256)
                total = lax.dot_general(
                    left[plane, rows, 0:G], operator[plane, 0], contract, preferred_element_type=jnp.float32
                ) + lax.dot_general(
                    left[plane, rows, G : 2 * G], operator[plane, 1], contract, preferred_element_type=jnp.float32
                )
                staged[turn, plane, group * 4 : group * 4 + 4] = total.astype(jnp.bfloat16).reshape(4, ROWS, 2, G)
                for entry in range(group * 4, group * 4 + 4):
                    pltpu.make_async_copy(
                        staged.at[turn, plane, entry], out.at[:, plane, index, entry], out_sems.at[turn]
                    ).start()
    for turn in range(len(types)):
        pltpu.make_async_copy(staged.at[turn], staged.at[turn], out_sems.at[turn]).wait()


def transform(types, ids, keep, ku, shared, own_last, far_last, lasts, previous):
    anywhere = pl.BlockSpec(memory_space=pl.ANY)
    in_hbm = pl.BlockSpec(memory_space=pltpu.HBM)
    scalars = pl.BlockSpec(memory_space=pltpu.SMEM)
    operands = [ids, keep, ku, *shared, *own_last, *far_last, *lasts]
    specs = [scalars, scalars, pl.BlockSpec(memory_space=pltpu.VMEM)] + [in_hbm] * (len(operands) - 3)
    aliases = {}
    if previous is not None:
        aliases = {len(operands): 0}
        operands.append(previous)
        specs.append(anywhere)

    def kernel(*refs):
        transform_kernel(types, *refs)

    count = len(types)
    return pl.pallas_call(
        kernel,
        out_shape=jax.ShapeDtypeStruct((ROWS, PLANES, RUN, 16, 2, G), jnp.bfloat16),
        in_specs=specs,
        out_specs=anywhere,
        input_output_aliases=aliases,
        scratch_shapes=[
            pltpu.VMEM((count, 2, 4, G, G), jnp.bfloat16),
            pltpu.VMEM((PLANES, 2, G, G), jnp.bfloat16),
            pltpu.VMEM((16, G, G), jnp.bfloat16),
            pltpu.VMEM((PLANES, 16 * 64, 2 * G), jnp.bfloat16),
            pltpu.VMEM((count, PLANES, 16, ROWS, 2, G), jnp.bfloat16),
            pltpu.SemaphoreType.DMA((count,)),
            pltpu.SemaphoreType.DMA,
            pltpu.SemaphoreType.DMA((count,)),
        ],
        compiler_params=pltpu.CompilerParams(vmem_limit_bytes=60 * 1024 * 1024),
        cost_estimate=pl.CostEstimate(flops=1_000_000, bytes_accessed=1_000_000, transcendentals=0),
        name="transform",
    )(*operands)


def after(value, *others):
    return lax.optimization_barrier((value, *others))[0]


def together(values):
    return list(lax.optimization_barrier(tuple(values)))


def choose(flags, yes, no):
    return jnp.where(flags[:, None, None, None], yes, no)


def body(jones, owner, mask, w_operator):
    wa = lax.axis_index("wa")
    grid = lax.axis_index("grid")
    core = wa & 1
    ids = jnp.stack([core, grid]).astype(jnp.int32)
    mine, other = pick(ids, owner, jones)

    kr, ki = w_operator[:, 0], w_operator[:, 1]
    plain = jnp.stack([kr, ki], 2).reshape(PLANES, 2 * ROWS, G)
    turned = jnp.stack([-ki, kr], 2).reshape(PLANES, 2 * ROWS, G)
    ku = jnp.concatenate([plain, turned], 1).reshape(PLANES * 4 * ROWS, G)
    keep = mask.reshape(RUN * 16)

    holder = owner[:RUN] >> 2
    rows = choose((holder & 1) == core, mine, swap_core(other))
    first = ZCLASSES[0][0] + core * (ZCLASSES[1][0] - ZCLASSES[0][0])
    apart = (holder ^ wa) & 6
    rows = choose(apart == 0, rows, swap_z(rows, 0))
    rows = choose((apart == 0) | (apart == first), rows, swap_z(rows, 1))
    rows, ku, keep, ids = together((rows, ku, keep, ids))

    halves = []
    for half in range(2):
        of_types = rows[:, 2 * half : 2 * half + 2]
        halves.append(jnp.concatenate([of_types[:1], w_operator[half : half + 1], of_types[1:]], 0))
    held = jnp.stack(halves)
    ring = [held, *together([swap_ring(held, turn) for turn in range(3)])]
    near = [jnp.stack([one[half] for one in ring]) for half in range(2)]
    next_blocks = together([swap_grid(near[half], half, 2) for half in range(2)])
    far_near = [swap_core(one) for one in near]
    far_next = [swap_core(one) for one in next_blocks]

    def send(members):
        return [jnp.concatenate([near[half][:, members], next_blocks[half][:, members]], 0) for half in range(2)]

    last = [swap_grid(one, half, 3) for half, one in enumerate(send(slice(0, 2)))]
    rest = send(slice(2, 4))
    moved = together((*last, *rest, *near, *next_blocks, *far_near, *far_next))
    lasts, rest, shared = [moved[:2]], moved[2:4], tuple(moved[4:])
    far_last = together([swap_core(last[:, :1]) for last in lasts[0]])
    lasts.append(together([swap_grid(one, half, 3) for half, one in enumerate(rest)]))
    result = transform((0,), ids, keep, ku, shared, lasts[0], far_last, (), None)
    far_last = [swap_core(after(last, result)) for last in lasts[1]]
    result = transform((1, 2), ids, keep, ku, shared, lasts[1], far_last, lasts[0], result)
    return result


def solution(mesh):
    return jax.shard_map(
        body,
        mesh=mesh,
        in_specs=(P("wa", None, None, "grid", None), P(), P(), P("wa", None, "grid", None)),
        out_specs=P("grid", "wa", None, None, None, None),
        check_vma=False,
    )
```

```python
import jax
import jax.numpy as jnp
import numpy as np
from jax import lax
from jax.experimental import pallas as pl
from jax.experimental.pallas import tpu as pltpu
from jax.sharding import PartitionSpec as P

RUN = 3
G = 512
ROWS = 32
PLANES = 2

CLASSES = (((1, 3, 4, 12), (1, 3, 12, 4)), ((4, 12, 1, 3), (4, 12, 3, 1)))
ZCLASSES = ((2, 6), (6, 2))

MEMBERS = (0, 2, 3)

PAIRS = ((0, 1), (0, 2), (0, 3), (1, 2), (1, 3), (2, 3))


def term(a, b):
    return 8 * (a // 2) + 4 * (b // 2) + 2 * (a % 2) + b % 2


def block_masks():
    table = np.zeros((2, 2, 16), np.int32)
    for core in range(2):
        for half in range(2):
            for block in range(16):
                for step in range(4):
                    if block >> step & 1:
                        table[core, half, block] ^= CLASSES[core][half][step]
    return table


MASKS = block_masks()


def exchange(value, wa_mask, grid_mask):
    perm = []
    for wa in range(8):
        for grid in range(16):
            core = wa % 2
            perm.append((wa * 16 + grid, (wa ^ wa_mask(core)) * 16 + (grid ^ grid_mask(core))))
    return lax.ppermute(value, ("wa", "grid"), perm)


def swap_core(value):
    return exchange(value, lambda core: 1, lambda core: 0)


def swap_z(value, step):
    return exchange(value, lambda core: ZCLASSES[core][step], lambda core: 0)


def swap_grid(value, half, step):
    return exchange(value, lambda core: 0, lambda core: CLASSES[core][half][step])


def swap_ring(value, turn):
    masks = [(one[0][0], one[0][1], one[0][0] ^ one[0][1])[turn] for one in CLASSES]
    return exchange(value, lambda core: 0, lambda core: masks[core])


def pick_kernel(owner, jones, mine, other, semaphore):
    core = lax.axis_index("wa") & 1
    copies = []
    for index in range(RUN):
        slot = owner[index] & 3
        for part, target in ((core, mine), (1 - core, other)):
            copies.append(
                pltpu.make_async_copy(jones.at[slot, :, part], target.at[index], semaphore.at[len(copies)])
            )
    for copy in copies:
        copy.start()
    for copy in copies:
        copy.wait()


def pick(owner, jones):
    shape = jax.ShapeDtypeStruct((RUN, 4, ROWS, G), jnp.bfloat16)
    scalars = pl.BlockSpec(memory_space=pltpu.SMEM)
    return pl.pallas_call(
        pick_kernel,
        out_shape=(shape, shape),
        in_specs=[scalars, pl.BlockSpec(memory_space=pl.ANY)],
        out_specs=(pl.BlockSpec(memory_space=pltpu.VMEM), pl.BlockSpec(memory_space=pltpu.VMEM)),
        scratch_shapes=[pltpu.SemaphoreType.DMA((RUN * 2,))],
        compiler_params=pltpu.CompilerParams(vmem_limit_bytes=61 * 1024 * 1024),
        name="pick",
    )(owner, jones)


def transform_kernel(types, *refs):
    ids, keep, ku = refs[:3]
    own = (refs[3:5], refs[5:7], refs[11:13])
    far = (refs[7:9], refs[9:11], refs[13:15])
    lasts = refs[15:17] if len(types) > 1 else refs[11:13]
    out, fields, operator, products, left, staged, field_sems, operator_sem, out_sems = refs[-9:]
    core, grid = ids[0], ids[1]

    def placed(half, block, near):
        masks = (int(MASKS[0, half, block]), int(MASKS[1, half, block]))
        chosen = jnp.where(core == 0, masks[0], masks[1]) if near else jnp.where(core == 0, masks[1], masks[0])
        return pl.ds(pl.multiple_of((grid ^ chosen) * ROWS, ROWS), ROWS)

    def block_of(group, half, block, member, last_member):
        if block < 8:
            return group[block // 4][half].at[block % 4, member]
        return group[2][half].at[block - 8, last_member]

    def load(turn):
        for half in range(2):
            for block in range(16):
                for near, source, part in ((True, own, core), (False, far, 1 - core)):
                    pltpu.make_async_copy(
                        block_of(source, half, block, MEMBERS[types[turn]], turn),
                        fields.at[turn, part, pl.ds(2 * half, 2), placed(half, block, near)],
                        field_sems.at[turn],
                    ).start()

    load(0)
    for half in range(2):
        for block in range(16):
            source = block_of(own, half, block, 1, 0) if block < 8 else lasts[half].at[block - 8, 1]
            pltpu.make_async_copy(source, operator.at[half, :, placed(half, block, True)], operator_sem).start()
    for turn in range(1, len(types)):
        load(turn)

    def multiply(turn, columns):
        for start in range(0, G, 16):
            rows = slice(start, start + 16)
            re = [fields[turn, 0, entry, rows, columns].astype(jnp.float32) for entry in range(4)]
            im = [fields[turn, 1, entry, rows, columns].astype(jnp.float32) for entry in range(4)]
            for a in range(4):
                products[a, rows, columns] = (re[a] * re[a] + im[a] * im[a]).astype(jnp.bfloat16)
            for at, (a, b) in enumerate(PAIRS):
                products[4 + 2 * at, rows, columns] = (re[a] * re[b] + im[a] * im[b]).astype(jnp.bfloat16)
                products[5 + 2 * at, rows, columns] = (im[a] * re[b] - re[a] * im[b]).astype(jnp.bfloat16)

    def put(plane, entry, columns, value, turned):
        rows = slice(entry * 64, entry * 64 + 64)
        left[plane, rows, columns] = value.astype(jnp.bfloat16)
        left[plane, rows, slice(columns.start + G, columns.stop + G)] = turned.astype(jnp.bfloat16)

    def first_pass(columns):
        def apply(field):
            return jnp.dot(ku[...], products[field, :, columns], preferred_element_type=jnp.float32)

        for a in range(4):
            whole = apply(a)
            for plane in range(PLANES):
                at = plane * 128
                put(plane, term(a, a), columns, whole[at : at + 64], whole[at + 64 : at + 128])
        for pair, (a, b) in enumerate(PAIRS):
            real, imag = apply(4 + 2 * pair), apply(5 + 2 * pair)
            for plane in range(PLANES):
                at = plane * 128
                xa, ya = real[at : at + 64], real[at + 64 : at + 128]
                xb, yb = imag[at : at + 64], imag[at + 64 : at + 128]
                put(plane, term(a, b), columns, xa + yb, ya - xb)
                put(plane, term(b, a), columns, xa - yb, ya + xb)

    chunks = [slice(start, start + 256) for start in range(0, G, 256)]
    contract = (((1,), (1,)), ((), ()))
    for turn, index in enumerate(types):
        pltpu.make_async_copy(fields.at[turn], fields.at[turn], field_sems.at[turn]).wait()
        multiply(turn, chunks[0])
        for step, chunk in enumerate(chunks):
            if step + 1 < len(chunks):
                multiply(turn, chunks[step + 1])
            first_pass(chunk)
        for entry in range(16):

            @pl.when(keep[index * 16 + entry] == 0)
            def _(entry=entry):
                left[:, entry * 64 : entry * 64 + 64] = jnp.zeros((PLANES, 64, 2 * G), jnp.bfloat16)

        if turn == 0:
            pltpu.make_async_copy(operator, operator, operator_sem).wait()
        for plane in range(PLANES):
            for group in range(4):
                rows = slice(group * 256, group * 256 + 256)
                total = lax.dot_general(
                    left[plane, rows, 0:G], operator[plane, 0], contract, preferred_element_type=jnp.float32
                ) + lax.dot_general(
                    left[plane, rows, G : 2 * G], operator[plane, 1], contract, preferred_element_type=jnp.float32
                )
                staged[turn, plane, group * 4 : group * 4 + 4] = total.astype(jnp.bfloat16).reshape(4, ROWS, 2, G)
                for entry in range(group * 4, group * 4 + 4):
                    pltpu.make_async_copy(
                        staged.at[turn, plane, entry], out.at[:, plane, index, entry], out_sems.at[turn]
                    ).start()
    for turn in range(len(types)):
        pltpu.make_async_copy(staged.at[turn], staged.at[turn], out_sems.at[turn]).wait()


def transform(types, ids, keep, ku, shared, own_last, far_last, lasts, previous):
    anywhere = pl.BlockSpec(memory_space=pl.ANY)
    in_hbm = pl.BlockSpec(memory_space=pltpu.HBM)
    scalars = pl.BlockSpec(memory_space=pltpu.SMEM)
    operands = [ids, keep, ku, *shared, *own_last, *far_last, *lasts]
    specs = [scalars, scalars, pl.BlockSpec(memory_space=pltpu.VMEM)] + [in_hbm] * (len(operands) - 3)
    aliases = {}
    if previous is not None:
        aliases = {len(operands): 0}
        operands.append(previous)
        specs.append(anywhere)

    def kernel(*refs):
        transform_kernel(types, *refs)

    count = len(types)
    return pl.pallas_call(
        kernel,
        out_shape=jax.ShapeDtypeStruct((ROWS, PLANES, RUN, 16, 2, G), jnp.bfloat16),
        in_specs=specs,
        out_specs=anywhere,
        input_output_aliases=aliases,
        scratch_shapes=[
            pltpu.VMEM((count, 2, 4, G, G), jnp.bfloat16),
            pltpu.VMEM((PLANES, 2, G, G), jnp.bfloat16),
            pltpu.VMEM((16, G, G), jnp.bfloat16),
            pltpu.VMEM((PLANES, 16 * 64, 2 * G), jnp.bfloat16),
            pltpu.VMEM((count, PLANES, 16, ROWS, 2, G), jnp.bfloat16),
            pltpu.SemaphoreType.DMA((count,)),
            pltpu.SemaphoreType.DMA,
            pltpu.SemaphoreType.DMA((count,)),
        ],
        compiler_params=pltpu.CompilerParams(vmem_limit_bytes=60 * 1024 * 1024),
        cost_estimate=pl.CostEstimate(flops=1_000_000, bytes_accessed=1_000_000, transcendentals=0),
        name="transform",
    )(*operands)


def after(value, *others):
    return lax.optimization_barrier((value, *others))[0]


def together(values):
    return list(lax.optimization_barrier(tuple(values)))


def choose(flags, yes, no):
    return jnp.where(flags[:, None, None, None], yes, no)


def body(jones, owner, mask, w_operator):
    wa = lax.axis_index("wa")
    grid = lax.axis_index("grid")
    core = wa & 1
    ids = jnp.stack([core, grid]).astype(jnp.int32)
    mine, other = pick(owner, jones)

    kr, ki = w_operator[:, 0], w_operator[:, 1]
    plain = jnp.stack([kr, ki], 2).reshape(PLANES, 2 * ROWS, G)
    turned = jnp.stack([-ki, kr], 2).reshape(PLANES, 2 * ROWS, G)
    ku = jnp.concatenate([plain, turned], 1).reshape(PLANES * 4 * ROWS, G)
    keep = mask.reshape(RUN * 16)

    holder = owner[:RUN] >> 2
    rows = choose((holder & 1) == core, mine, swap_core(other))
    first = ZCLASSES[0][0] + core * (ZCLASSES[1][0] - ZCLASSES[0][0])
    apart = (holder ^ wa) & 6
    rows = choose(apart == 0, rows, swap_z(rows, 0))
    rows = choose((apart == 0) | (apart == first), rows, swap_z(rows, 1))
    rows, ku, keep, ids = together((rows, ku, keep, ids))

    halves = []
    for half in range(2):
        of_types = rows[:, 2 * half : 2 * half + 2]
        halves.append(jnp.concatenate([of_types[:1], w_operator[half : half + 1], of_types[1:]], 0))
    held = jnp.stack(halves)
    ring = [held, *together([swap_ring(held, turn) for turn in range(3)])]
    near = [jnp.stack([one[half] for one in ring]) for half in range(2)]
    next_blocks = together([swap_grid(near[half], half, 2) for half in range(2)])
    far_near = [swap_core(one) for one in near]
    far_next = [swap_core(one) for one in next_blocks]

    def send(members):
        return [jnp.concatenate([near[half][:, members], next_blocks[half][:, members]], 0) for half in range(2)]

    last = [swap_grid(one, half, 3) for half, one in enumerate(send(slice(0, 2)))]
    rest = send(slice(2, 4))
    others = [swap_grid(one, half, 3) for half, one in enumerate(rest)]
    moved = together((*last, *near, *next_blocks, *far_near, *far_next))
    lasts, shared = [moved[:2]], tuple(moved[2:])
    far_last = together([swap_core(last[:, :1]) for last in lasts[0]])
    result = transform((0,), ids, keep, ku, shared, lasts[0], far_last, (), None)
    *others, result = together((*others, result))
    lasts.append(others)
    far_last = [swap_core(last) for last in others]
    result = transform((1, 2), ids, keep, ku, shared, lasts[1], far_last, lasts[0], result)
    return result


def solution(mesh):
    return jax.shard_map(
        body,
        mesh=mesh,
        in_specs=(P("wa", None, None, "grid", None), P(), P(), P("wa", None, "grid", None)),
        out_specs=P("grid", "wa", None, None, None, None),
        check_vma=False,
    )
```
